32 devices in a mesh: grp: 2 (over y), bits: 4 (over z), tgt: 2 (over x), sub: 2 (over core).
Axes of the slice: x: 2, y: 2, z: 4, core: 2. Of those that a mesh axis runs over, the one named last changes fastest.
Arguments:
- coefficients: bfloat16 [16, 8192, 128], P(('grp', 'bits', 'sub'), 'tgt'), parts along dimension 0, may hold values from -6 to 6
- patterns: int32 [2, 16, 8192], P(None, ('grp', 'bits', 'sub'), 'tgt'), parts along dimension 1, may hold values from 0 to 65535
- blocks: bfloat16 [2, 16, 2048, 128], P(None, ('grp', 'bits', 'sub')), parts along dimension 1, may hold values from -0.1875 to 0.1875
- box_index: int32 [16], P(('grp', 'bits', 'sub')), parts along dimension 0, may hold values from 0 to 4095
- target_index: int32 [16384], P(('grp', 'tgt')), parts along dimension 0, may hold values from 0 to 4095
- partner_bits: int32 [4], P('grp'), parts along dimension 0, may hold values from 0 to 2, as said below
- evaluation: bfloat16 [128, 8192], replicated, may hold values from -0.0625 to 0.0625
Outputs:
- values: float32 [16, 128, 128], P(('grp', 'bits', 'sub'), 'tgt'), parts along dimension 0
The draws below stay inside these ranges and needn't reach their ends.
There are 2 independent parts, one for each index of `grp`. The reference program is written for one: setup_inputs(seed, part) draws one part's arguments, and reference() takes and returns one part's arrays. A program takes and returns all parts, laid end to end along the dimension named above; an argument that names none is the same for every part. Nothing has to cross between parts.
Inputs may be any that keep to these rules, and one draw needn't show every extreme that they name: `partner_bits`: two different bits of a box number; the highest bit 3 - 1 is always one of them.
All inputs are finite; a program needn't handle non-finite values.
Results may differ from the reference program's by a relative error of at most 0.0042.
Values may be sent and summed in bfloat16 or wider, within the bound.
A program may use at most 64 MiB of HBM per device.

```python
import math
import jax
import jax.numpy as jnp
from jax import lax

RANK = 128
NPAT = 8
LEVELS = 2
POINTS = 128
NB = 8
LOG_BOX = 3
M = 8192


def draw_partner_bits(key, part):
    key = jax.random.fold_in(key, 7)
    first_key, second_key = jax.random.split(key)
    highest = LOG_BOX - 1
    other = jax.random.randint(first_key, (), 0, highest).astype(jnp.int32)
    coin = jax.random.randint(second_key, (), 0, 2).astype(jnp.int32)
    place = (coin + jnp.asarray(part).astype(jnp.int32)) % 2
    top_value = jnp.int32(highest)
    return jnp.where(place == 0, jnp.stack([top_value, other]), jnp.stack([other, top_value])).astype(jnp.int32)


def set_ends(result, own_key, low, high):
    index_at = [jax.random.randint(jax.random.fold_in(own_key, axis), (), 0, length) for axis, length in enumerate(result.shape)]
    longest = result.shape.index(max(result.shape))
    beside = index_at[:longest] + [(index_at[longest] + 1) % result.shape[longest]] + index_at[longest + 1:]
    return result.at[tuple(index_at)].set(low).at[tuple(beside)].set(high)


def block_scale(stream_key, extent, cuts, low, high):
    level = 1.0
    for dim, shards_of in cuts:
        steps = jax.random.uniform(jax.random.fold_in(jax.random.fold_in(stream_key, 6), dim), (shards_of,), jnp.float32, low / len(cuts), high / len(cuts))
        level = level * jnp.repeat(jnp.exp(steps), extent[dim] // shards_of).reshape((-1,) + (1,) * (len(extent) - 1 - dim))
    return level


def noise(rng, extent, deviation, bound, shards=(), kind=jnp.bfloat16):
    gain = block_scale(rng, extent, shards, -0.22, 0.18) if shards else 1.0
    array = jax.random.normal(rng, extent, jnp.float32) * deviation * gain
    return jnp.minimum(jnp.maximum(array, -bound), bound).astype(kind)


def setup_inputs(seed: int = 0, part: int = 0) -> dict:
    keys = jax.random.split(jax.random.key(seed), 8)
    own_keys = jax.random.split(jax.random.fold_in(keys[7], part), 8)
    return {
        "coefficients": noise(own_keys[0], (NB, M, RANK), 1.0, 6.0, ((0, 8), (1, 2))),
        "patterns": set_ends(jax.random.randint(own_keys[1], (LEVELS, NB, M), 0, 65536), jax.random.fold_in(own_keys[1], 1), 0, 65535).astype(jnp.int32),
        "blocks": noise(own_keys[2], (LEVELS, NB, 2 * NPAT * RANK, RANK), (NPAT * RANK) ** -0.5, 0.1875, ((1, 8),)),
        "box_index": set_ends(jax.random.randint(own_keys[3], (NB,), 0, 4096), jax.random.fold_in(own_keys[3], 1), 0, 4095).astype(jnp.int32),
        "target_index": set_ends(jax.random.randint(own_keys[4], (M,), 0, 4096), jax.random.fold_in(own_keys[4], 1), 0, 4095).astype(jnp.int32),
        "partner_bits": draw_partner_bits(jax.random.fold_in(jax.random.fold_in(keys[7], part), 71), part),
        "evaluation": noise(keys[6], (POINTS, M), M ** -0.5, 0.0625),
    }


def rotate_rows(mixed, source_box, targets, level):
    turns = (targets * source_box * (level + 1)) % 4096
    phase = turns.astype(jnp.float32) * (2.0 * math.pi / 4096.0)
    half_width = mixed.shape[1] // 2
    cosine_part = mixed[:, :half_width]
    sine_part = mixed[:, half_width:]
    cos_phase = jnp.cos(phase)[:, None]
    sin_phase = jnp.sin(phase)[:, None]
    first = cosine_part * cos_phase - sine_part * sin_phase
    second = cosine_part * sin_phase + sine_part * cos_phase
    return jnp.concatenate([first, second], axis=1).astype(jnp.bfloat16)


def level_box(own_rows, partner_rows, pattern_row, weight, source_box, targets, level):
    row_count, width = own_rows.shape
    shifts = jnp.arange(2 * NPAT, dtype=jnp.int32)
    masks = ((pattern_row[:, None] >> shifts[None, :]) & 1).astype(jnp.float32)
    own_copies = jnp.broadcast_to(own_rows.astype(jnp.float32)[:, None, :], (row_count, NPAT, width))
    partner_copies = jnp.broadcast_to(partner_rows.astype(jnp.float32)[:, None, :], (row_count, NPAT, width))
    stacked = jnp.concatenate([own_copies, partner_copies], axis=1) * masks[:, :, None]
    mixed = jnp.dot(stacked.reshape(row_count, 2 * NPAT * width), weight.astype(jnp.float32), precision=lax.Precision.HIGHEST)
    return rotate_rows(mixed, source_box, targets, level)


def reference(coefficients, patterns, blocks, box_index, target_index, partner_bits, evaluation):
    current = coefficients
    box_ids = jnp.arange(NB, dtype=jnp.int32)
    for level in range(LEVELS):
        partner_ids = box_ids ^ jnp.left_shift(jnp.int32(1), partner_bits[level].astype(jnp.int32))
        partner_state = current[partner_ids]

        def one_box(items, level=level):
            own_rows, partner_rows, pattern_row, weight, source_box = items
            return level_box(own_rows, partner_rows, pattern_row, weight, source_box, target_index, level)

        current = lax.map(one_box, (current, partner_state, patterns[level], blocks[level], box_index))

    def evaluate(rows):
        return jnp.dot(evaluation, rows, preferred_element_type=jnp.float32)

    return lax.map(evaluate, current)
```

```python
from functools import partial
import math

import jax
import jax.numpy as jnp
from jax import lax
from jax.experimental import pallas as pl
from jax.experimental.pallas import tpu as pltpu
from jax.sharding import PartitionSpec as P

GROUP = 128
CHUNKS = 8
LAG = 2


def swap_bit(block, axis, bit):
    count = lax.axis_size(axis)
    return lax.ppermute(block, axis, [(i, i ^ (1 << bit)) for i in range(count)])


def column_of(row, rows, width):
    return jnp.transpose(jnp.broadcast_to(row, (width, rows)))


def mix_group(own, partner, pattern_row, weight, cos_row, sin_row):
    rows, width = own.shape
    terms = weight.shape[0] // width
    half = width // 2
    pattern = column_of(pattern_row, rows, width)
    own32 = own.astype(jnp.float32)
    partner32 = partner.astype(jnp.float32)
    parts = []
    for k in range(terms):
        source = own32 if k < terms // 2 else partner32
        parts.append(jnp.where((pattern & (1 << k)) != 0, source, 0.0).astype(jnp.bfloat16))
    stacked = jnp.concatenate(parts, axis=1)
    mixed = jnp.dot(stacked, weight, preferred_element_type=jnp.float32)
    cos_all = column_of(cos_row, rows, width)
    sin_all = column_of(sin_row, rows, width)
    lane = lax.broadcasted_iota(jnp.int32, (rows, width), 1)
    signed = jnp.where(lane < half, -sin_all, sin_all)
    return (mixed * cos_all + pltpu.roll(mixed, half, 1) * signed).astype(jnp.bfloat16)


def step_kernel(first, second, *refs):
    refs = list(refs)
    patterns, trig, weights = refs[:3]
    del refs[:3]
    if first is not None:
        own0, partner0 = refs[:2]
        del refs[:2]
    if second is not None:
        own1, partner1, evaluation, total_in = refs[:4]
        del refs[:4]
    if first is not None:
        state1 = refs.pop(0)
        groups = own0.shape[0] // GROUP
        for g in range(groups):
            at = first * groups + g
            rows = slice(g * GROUP, (g + 1) * GROUP)
            state1[rows, :] = mix_group(
                own0[rows, :], partner0[rows, :], patterns[0, at:at + 1, :], weights[0],
                trig[0, 0, at:at + 1, :], trig[0, 1, at:at + 1, :])
    if second is not None:
        total = refs.pop(0)
        groups = own1.shape[0] // GROUP
        out = []
        for g in range(groups):
            at = second * groups + g
            rows = slice(g * GROUP, (g + 1) * GROUP)
            out.append(mix_group(
                own1[rows, :], partner1[rows, :], patterns[1, at:at + 1, :], weights[1],
                trig[1, 0, at:at + 1, :], trig[1, 1, at:at + 1, :]))
        total[...] = total_in[...] + jnp.dot(
            evaluation[...], jnp.concatenate(out, axis=0), preferred_element_type=jnp.float32)


def step(first, second, chunk_rows, patterns, trig, weights, own0=None, partner0=None,
         own1=None, partner1=None, evaluation=None, total=None):
    width = weights.shape[-1]

    def full(array):
        return pl.BlockSpec(array.shape, lambda i, n=array.ndim: (0,) * n)

    operands = [patterns, trig, weights]
    in_specs = [full(a) for a in operands]
    out_shape, out_specs = [], []
    flops = 0
    if first is not None:
        operands += [own0, partner0]
        in_specs += [pl.BlockSpec((chunk_rows, width), lambda i: (first, 0)), full(partner0)]
        out_shape.append(jax.ShapeDtypeStruct((chunk_rows, width), jnp.bfloat16))
        out_specs.append(pl.BlockSpec((chunk_rows, width), lambda i: (0, 0)))
        flops += 2 * chunk_rows * weights.shape[1] * width
    if second is not None:
        points = evaluation.shape[0]
        operands += [own1, partner1, evaluation, total]
        in_specs += [full(own1), full(partner1),
                     pl.BlockSpec((points, chunk_rows), lambda i: (0, second)), full(total)]
        out_shape.append(jax.ShapeDtypeStruct(total.shape, jnp.float32))
        out_specs.append(full(total))
        flops += 2 * chunk_rows * (weights.shape[1] + points) * width
    return pl.pallas_call(
        partial(step_kernel, first, second),
        grid=(1,),
        out_shape=out_shape,
        in_specs=in_specs,
        out_specs=out_specs,
        cost_estimate=pl.CostEstimate(flops=flops, bytes_accessed=2 << 20, transcendentals=0),
        compiler_params=pltpu.CompilerParams(vmem_limit_bytes=32 << 20),
    )(*operands)


def run_levels(bits, current, patterns, trig, weights, evaluation):
    rows, width = current.shape
    chunk_rows = rows // CHUNKS
    axes = ("bits", "sub")
    arrived0 = [swap_bit(current[c * chunk_rows:(c + 1) * chunk_rows], axes, bits[0]) for c in range(CHUNKS)]
    states, arrived1 = {}, {}
    total = jnp.zeros((evaluation.shape[0], width), jnp.float32)
    for c in range(CHUNKS + LAG):
        first = c if c < CHUNKS else None
        second = c - LAG if c >= LAG else None
        given = {}
        if first is not None:
            given.update(own0=current, partner0=arrived0[first])
        if second is not None:
            given.update(own1=states.pop(second), partner1=arrived1.pop(second),
                         evaluation=evaluation, total=total)
        out = list(step(first, second, chunk_rows, patterns, trig, weights, **given))
        if first is not None:
            states[first] = out.pop(0)
            arrived1[first] = swap_bit(states[first], axes, bits[1])
        if second is not None:
            total = out.pop(0)
    return total


def body(coefficients, patterns, blocks, box_index, target_index, partner_bits, evaluation):
    current = coefficients[0]
    rows = current.shape[0]
    levels = patterns.shape[0]
    weights = blocks[:, 0]
    pattern_rows = patterns[:, 0].reshape(levels, rows // GROUP, GROUP)
    targets = target_index.reshape(1, rows // GROUP, GROUP)
    scale = jnp.arange(1, levels + 1, dtype=jnp.int32)[:, None, None]
    turns = (targets * box_index[0] * scale) % 4096
    phase = turns.astype(jnp.float32) * (2.0 * math.pi / 4096.0)
    trig = jnp.stack([jnp.cos(phase), jnp.sin(phase)], axis=1)
    mine = lax.axis_index("tgt")
    local_eval = lax.dynamic_slice_in_dim(evaluation, mine * rows, rows, 1)

    top = lax.axis_size(("bits", "sub")).bit_length() - 2
    pairs = [(top, other) for other in range(top)] + [(other, top) for other in range(top)]
    which = jnp.where(partner_bits[0] == top, partner_bits[1], top + partner_bits[0])
    partial_values = lax.switch(
        which, [partial(run_levels, pair) for pair in pairs],
        current, pattern_rows, trig, weights, local_eval)

    spread = lax.axis_size("tgt")
    points = evaluation.shape[0] // spread
    pieces = partial_values.reshape(spread, points, -1)
    result = lax.dynamic_index_in_dim(pieces, mine, 0, keepdims=False)
    for apart in range(1, spread):
        away = lax.dynamic_index_in_dim(pieces, (mine + apart) % spread, 0, keepdims=False)
        result = result + lax.ppermute(away, "tgt", [(i, (i + apart) % spread) for i in range(spread)])
    return result[None]


def solution(mesh):
    in_specs = (
        P(("grp", "bits", "sub"), "tgt", None),
        P(None, ("grp", "bits", "sub"), "tgt"),
        P(None, ("grp", "bits", "sub"), None, None),
        P(("grp", "bits", "sub")),
        P(("grp", "tgt")),
        P("grp"),
        P(),
    )
    out_specs = P(("grp", "bits", "sub"), "tgt", None)
    return jax.shard_map(body, mesh=mesh, in_specs=in_specs, out_specs=out_specs, check_vma=False)
```

```python
from functools import partial
import math

import jax
import jax.numpy as jnp
from jax import lax
from jax.experimental import pallas as pl
from jax.experimental.pallas import tpu as pltpu
from jax.sharding import PartitionSpec as P

GROUP = 128
CHUNK = 256
LAG = 4
MESH = pl.DeviceIdType.MESH


def column_of(row, rows, width):
    return jnp.transpose(jnp.broadcast_to(row, (width, rows)))


def cos_sin(turns):
    quarter = (turns + 512) >> 10
    x = (turns - (quarter << 10)).astype(jnp.float32) * (2.0 * math.pi / 4096.0)
    y = x * x
    s = x * (1.0 + y * (-1.0 / 6 + y * (1.0 / 120 + y * (-1.0 / 5040 + y * (1.0 / 362880)))))
    c = 1.0 + y * (-0.5 + y * (1.0 / 24 + y * (-1.0 / 720 + y * (1.0 / 40320 - y * (1.0 / 3628800)))))
    odd = (quarter & 1) == 1
    cos = jnp.where(odd, s, c)
    sin = jnp.where(odd, c, s)
    turn = quarter & 3
    cos = jnp.where((turn == 1) | (turn == 2), -cos, cos)
    sin = jnp.where((turn == 2) | (turn == 3), -sin, sin)
    return cos, sin


def mix(own, partner, pattern, weight, cos, sin):
    rows, width = own.shape
    terms = weight.shape[0] // width
    half = width // 2
    own32 = own.astype(jnp.float32)
    partner32 = partner.astype(jnp.float32)
    parts = []
    for k in range(terms):
        source = own32 if k < terms // 2 else partner32
        parts.append(jnp.where((pattern & (1 << k)) != 0, source, 0.0).astype(jnp.bfloat16))
    mixed = jnp.dot(jnp.concatenate(parts, axis=1), weight, preferred_element_type=jnp.float32)
    lane = lax.broadcasted_iota(jnp.int32, (rows, width), 1)
    signed = jnp.where(lane < half, -sin, sin)
    return (mixed * cos + pltpu.roll(mixed, half, 1) * signed).astype(jnp.bfloat16)


def kernel(top_first, sizes, box, bits, patterns, targets, weights, state0, evaluation, out,
           state1, arrived, trig, points_eval, total, sums,
           send_sem, recv_sem, eval_sem, sum_send, sum_recv):
    grp_n, bits_n, tgt_n, sub_n = sizes
    rows, width = state0.shape
    chunks = rows // CHUNK
    groups = CHUNK // GROUP
    levels = weights.shape[0]
    boxes = bits_n * sub_n
    lower = boxes.bit_length() - 2
    grp, tgt = lax.axis_index("grp"), lax.axis_index("tgt")
    me = lax.axis_index("bits") * sub_n + lax.axis_index("sub")
    if all(top_first):
        first = 1
    elif not any(top_first):
        first = 0
    else:
        first = sum(jnp.where(grp == g, 1, 0) for g in range(grp_n) if top_first[g])

    def across(stride):
        other = me + stride - 2 * stride * ((me // stride) % 2)
        return (grp, other // sub_n, tgt, other % sub_n)

    def at_tgt(t):
        return (grp, lax.axis_index("bits"), t, lax.axis_index("sub"))

    peers = [across(1 << j) for j in range(lower + 1)]
    peers += [at_tgt((tgt + d) % tgt_n) for d in range(1, tgt_n)]
    barrier = pltpu.get_barrier_semaphore()
    for peer in peers:
        pl.semaphore_signal(barrier, inc=1, device_id=peer, device_id_type=MESH)

    load_eval = pltpu.make_async_copy(
        evaluation.at[:, pl.ds(pl.multiple_of(tgt * rows, rows), rows)], points_eval, eval_sem)
    load_eval.start()

    pl.semaphore_wait(barrier, len(peers))

    def is_top(level):
        return first if level == 0 else 1 - first

    def copy(level, slot, c):
        source = state0 if level == 0 else state1
        span = pl.ds(pl.multiple_of(c * CHUNK, CHUNK), CHUNK)
        stride = 1 << slot
        if slot == 0:
            stride = 1 + is_top(level) * ((1 << lower) - 1)
        return pltpu.make_async_remote_copy(
            src_ref=source.at[span],
            dst_ref=arrived.at[level, slot, span],
            send_sem=send_sem.at[level, slot, c],
            recv_sem=recv_sem.at[level, slot, c],
            device_id=across(stride),
            device_id_type=MESH,
        )

    def each_copy(level, c, act):
        act(copy(level, 0, c))
        top = is_top(level)
        if isinstance(top, int):
            if not top:
                for slot in range(1, lower):
                    act(copy(level, slot, c))
        elif lower > 1:
            @pl.when(top == 0)
            def _():
                for slot in range(1, lower):
                    act(copy(level, slot, c))

    @pl.loop(0, chunks)
    def _(c):
        each_copy(0, c, lambda k: k.start())

    for level in range(levels):
        turns = (targets[...] * (box[0] * (level + 1))) & 4095
        cos, sin = cos_sin(turns)
        trig[level, 0] = cos
        trig[level, 1] = sin
    total[...] = jnp.zeros_like(total)
    load_eval.wait()

    def advance(level, c):
        each_copy(level, c, lambda k: k.wait_recv())
        span = pl.ds(pl.multiple_of(c * CHUNK, CHUNK), CHUNK)
        own = (state0 if level == 0 else state1)[span, :]
        partner = arrived[level, 0, span, :]
        for slot in range(1, lower):
            partner = jnp.where(bits[level] == slot, arrived[level, slot, span, :], partner)

        def column(ref, *lead):
            return jnp.concatenate(
                [column_of(ref[(*lead, pl.ds(c * groups + g, 1), slice(None))], GROUP, width)
                 for g in range(groups)], axis=0)

        return mix(own, partner, column(patterns, level), weights[level],
                   column(trig, level, 0), column(trig, level, 1))

    @pl.loop(0, chunks + LAG)
    def _(i):
        @pl.when(i < chunks)
        def _():
            state1[pl.ds(pl.multiple_of(i * CHUNK, CHUNK), CHUNK), :] = advance(0, i)
            each_copy(1, i, lambda k: k.start())

        @pl.when(i >= LAG)
        def _():
            c = i - LAG
            span = pl.ds(pl.multiple_of(c * CHUNK, CHUNK), CHUNK)
            total[...] += jnp.dot(points_eval[:, span], advance(1, c), preferred_element_type=jnp.float32)

    piece = out.shape[0]

    def sum_copy(d):
        peer = (tgt + d) % tgt_n
        return pltpu.make_async_remote_copy(
            src_ref=total.at[pl.ds(pl.multiple_of(peer * piece, piece), piece)],
            dst_ref=sums.at[d - 1],
            send_sem=sum_send.at[d - 1],
            recv_sem=sum_recv.at[d - 1],
            device_id=at_tgt(peer),
            device_id_type=MESH,
        )

    for d in range(1, tgt_n):
        sum_copy(d).start()

    @pl.loop(0, chunks)
    def _(c):
        for level in range(levels):
            each_copy(level, c, lambda k: k.wait_send())

    result = total[pl.ds(pl.multiple_of(tgt * piece, piece), piece), :]
    for d in range(1, tgt_n):
        sum_copy(d).wait()
        result = result + sums[d - 1]
    out[...] = result


def run(top_first, number, sizes, box, bits, patterns, targets, weights, state, evaluation):
    rows, width = state.shape
    levels = weights.shape[0]
    points = evaluation.shape[0]
    lower = (sizes[1] * sizes[3]).bit_length() - 2
    slots = max(lower, 1)
    chunks = rows // CHUNK
    others = max(sizes[2] - 1, 1)
    smem = pl.BlockSpec(memory_space=pltpu.SMEM)
    vmem = pl.BlockSpec(memory_space=pltpu.VMEM)
    return pl.pallas_call(
        partial(kernel, top_first, sizes),
        out_shape=jax.ShapeDtypeStruct((points // sizes[2], width), jnp.float32),
        in_specs=[smem, smem, vmem, vmem, vmem, vmem, pl.BlockSpec(memory_space=pl.ANY)],
        out_specs=vmem,
        scratch_shapes=[
            pltpu.VMEM((rows, width), jnp.bfloat16),
            pltpu.VMEM((levels, slots, rows, width), jnp.bfloat16),
            pltpu.VMEM((levels, 2, rows // GROUP, GROUP), jnp.float32),
            pltpu.VMEM((points, rows), jnp.bfloat16),
            pltpu.VMEM((points, width), jnp.float32),
            pltpu.VMEM((others, points // sizes[2], width), jnp.float32),
            pltpu.SemaphoreType.DMA((levels, slots, chunks)),
            pltpu.SemaphoreType.DMA((levels, slots, chunks)),
            pltpu.SemaphoreType.DMA,
            pltpu.SemaphoreType.DMA((others,)),
            pltpu.SemaphoreType.DMA((others,)),
        ],
        cost_estimate=pl.CostEstimate(
            flops=2 * levels * rows * weights.shape[1] * width, bytes_accessed=8 << 20, transcendentals=0),
        compiler_params=pltpu.CompilerParams(
            collective_id=number, has_side_effects=True, vmem_limit_bytes=40 << 20),
    )(box, bits, patterns, targets, weights, state, evaluation)


def body(sizes, coefficients, patterns, blocks, box_index, target_index, partner_bits, evaluation):
    state = coefficients[0]
    rows = state.shape[0]
    levels = patterns.shape[0]
    pattern_rows = patterns.reshape(levels, rows // GROUP, GROUP)
    targets = target_index.reshape(rows // GROUP, GROUP)

    grp_n = sizes[0]
    mine = lax.axis_index("grp")
    top = (sizes[1] * sizes[3]).bit_length() - 2

    def flag(bits):
        return (bits[0] == top).astype(jnp.int32)

    which = flag(partner_bits) << mine
    for apart in range(1, grp_n):
        theirs = lax.ppermute(partner_bits, "grp", [(g, (g + apart) % grp_n) for g in range(grp_n)])
        which = which + (flag(theirs) << ((mine - apart) % grp_n))
    variants = [tuple(bool(v >> g & 1) for g in range(grp_n)) for v in range(1 << grp_n)]
    result = lax.switch(
        which, [partial(run, variant, v, sizes) for v, variant in enumerate(variants)],
        box_index, partner_bits, pattern_rows, targets, blocks[:, 0], state, evaluation)
    return result[None]


def solution(mesh):
    sizes = tuple(mesh.shape[name] for name in ("grp", "bits", "tgt", "sub"))
    in_specs = (
        P(("grp", "bits", "sub"), "tgt", None),
        P(None, ("grp", "bits", "sub"), "tgt"),
        P(None, ("grp", "bits", "sub"), None, None),
        P(("grp", "bits", "sub")),
        P(("grp", "tgt")),
        P("grp"),
        P(),
    )
    out_specs = P(("grp", "bits", "sub"), "tgt", None)
    return jax.shard_map(
        partial(body, sizes), mesh=mesh, in_specs=in_specs, out_specs=out_specs, check_vma=False)
```

```python
from functools import partial
import math

import jax
import jax.numpy as jnp
from jax import lax
from jax.experimental import pallas as pl
from jax.experimental.pallas import tpu as pltpu
from jax.sharding import PartitionSpec as P

GROUP = 128
CHUNK = 256
LAG = 2
WINDOW = 3
MESH = pl.DeviceIdType.MESH


def column_of(row, rows, width):
    return jnp.transpose(jnp.broadcast_to(row, (width, rows)))


def cos_sin(turns):
    quarter = (turns + 512) >> 10
    x = (turns - (quarter << 10)).astype(jnp.float32) * (2.0 * math.pi / 4096.0)
    y = x * x
    s = x * (1.0 + y * (-1.0 / 6 + y * (1.0 / 120 + y * (-1.0 / 5040 + y * (1.0 / 362880)))))
    c = 1.0 + y * (-0.5 + y * (1.0 / 24 + y * (-1.0 / 720 + y * (1.0 / 40320 - y * (1.0 / 3628800)))))
    odd = (quarter & 1) == 1
    cos = jnp.where(odd, s, c)
    sin = jnp.where(odd, c, s)
    turn = quarter & 3
    cos = jnp.where((turn == 1) | (turn == 2), -cos, cos)
    sin = jnp.where((turn == 2) | (turn == 3), -sin, sin)
    return cos, sin


def mix(own, partner, pattern, weight, cos, sin):
    rows, width = own.shape
    terms = weight.shape[0] // width
    half = width // 2
    own32 = own.astype(jnp.float32)
    partner32 = partner.astype(jnp.float32)
    parts = []
    for k in range(terms):
        source = own32 if k < terms // 2 else partner32
        parts.append(jnp.where((pattern & (1 << k)) != 0, source, 0.0).astype(jnp.bfloat16))
    mixed = jnp.dot(jnp.concatenate(parts, axis=1), weight, preferred_element_type=jnp.float32)
    lane = lax.broadcasted_iota(jnp.int32, (rows, width), 1)
    signed = jnp.where(lane < half, -sin, sin)
    return (mixed * cos + pltpu.roll(mixed, half, 1) * signed).astype(jnp.bfloat16)


def kernel(top_first, sizes, box, bits, patterns, targets, weights, state0, evaluation, out,
           state1, arrived, trig, points_eval, total, sums,
           send_sem, recv_sem, eval_sem, sum_send, sum_recv):
    grp_n, bits_n, tgt_n, sub_n = sizes
    rows, width = state0.shape
    chunks = rows // CHUNK
    groups = CHUNK // GROUP
    levels = weights.shape[0]
    boxes = bits_n * sub_n
    lower = boxes.bit_length() - 2
    grp, tgt = lax.axis_index("grp"), lax.axis_index("tgt")
    me = lax.axis_index("bits") * sub_n + lax.axis_index("sub")
    if all(top_first):
        first = 1
    elif not any(top_first):
        first = 0
    else:
        first = sum(jnp.where(grp == g, 1, 0) for g in range(grp_n) if top_first[g])

    def across(stride):
        other = me + stride - 2 * stride * ((me // stride) % 2)
        return (grp, other // sub_n, tgt, other % sub_n)

    def at_tgt(t):
        return (grp, lax.axis_index("bits"), t, lax.axis_index("sub"))

    peers = [across(1 << j) for j in range(lower + 1)]
    peers += [at_tgt((tgt + d) % tgt_n) for d in range(1, tgt_n)]
    barrier = pltpu.get_barrier_semaphore()
    for peer in peers:
        pl.semaphore_signal(barrier, inc=1, device_id=peer, device_id_type=MESH)

    load_eval = pltpu.make_async_copy(
        evaluation.at[:, pl.ds(pl.multiple_of(tgt * rows, rows), rows)], points_eval, eval_sem)
    load_eval.start()

    pl.semaphore_wait(barrier, len(peers))

    def is_top(level):
        return first if level == 0 else 1 - first

    def copy(level, slot, c):
        source = state0 if level == 0 else state1
        span = pl.ds(pl.multiple_of(c * CHUNK, CHUNK), CHUNK)
        stride = 1 << slot
        if slot == 0:
            stride = 1 + is_top(level) * ((1 << lower) - 1)
        return pltpu.make_async_remote_copy(
            src_ref=source.at[span],
            dst_ref=arrived.at[level, slot, span],
            send_sem=send_sem.at[level, slot, c],
            recv_sem=recv_sem.at[level, slot, c],
            device_id=across(stride),
            device_id_type=MESH,
        )

    def each_copy(level, c, act):
        act(copy(level, 0, c))
        top = is_top(level)
        if isinstance(top, int):
            if not top:
                for slot in range(1, lower):
                    act(copy(level, slot, c))
        elif lower > 1:
            @pl.when(top == 0)
            def _():
                for slot in range(1, lower):
                    act(copy(level, slot, c))

    @pl.loop(0, min(WINDOW, chunks))
    def _(c):
        each_copy(0, c, lambda k: k.start())

    for level in range(levels):
        turns = (targets[...] * (box[0] * (level + 1))) & 4095
        cos, sin = cos_sin(turns)
        trig[level, 0] = cos
        trig[level, 1] = sin
    total[...] = jnp.zeros_like(total)
    load_eval.wait()

    def advance(level, c):
        each_copy(level, c, lambda k: k.wait_recv())
        if level == 0:
            @pl.when(c + WINDOW < chunks)
            def _():
                each_copy(0, c + WINDOW, lambda k: k.start())
        span = pl.ds(pl.multiple_of(c * CHUNK, CHUNK), CHUNK)
        own = (state0 if level == 0 else state1)[span, :]
        partner = arrived[level, 0, span, :]
        for slot in range(1, lower):
            partner = jnp.where(bits[level] == slot, arrived[level, slot, span, :], partner)

        def column(ref, *lead):
            return jnp.concatenate(
                [column_of(ref[(*lead, pl.ds(c * groups + g, 1), slice(None))], GROUP, width)
                 for g in range(groups)], axis=0)

        return mix(own, partner, column(patterns, level), weights[level],
                   column(trig, level, 0), column(trig, level, 1))

    @pl.loop(0, chunks + LAG)
    def _(i):
        @pl.when(i < chunks)
        def _():
            state1[pl.ds(pl.multiple_of(i * CHUNK, CHUNK), CHUNK), :] = advance(0, i)
            each_copy(1, i, lambda k: k.start())

        @pl.when(i >= LAG)
        def _():
            c = i - LAG
            span = pl.ds(pl.multiple_of(c * CHUNK, CHUNK), CHUNK)
            total[...] += jnp.dot(points_eval[:, span], advance(1, c), preferred_element_type=jnp.float32)

    piece = out.shape[0]

    def sum_copy(d):
        peer = (tgt + d) % tgt_n
        return pltpu.make_async_remote_copy(
            src_ref=total.at[pl.ds(pl.multiple_of(peer * piece, piece), piece)],
            dst_ref=sums.at[d - 1],
            send_sem=sum_send.at[d - 1],
            recv_sem=sum_recv.at[d - 1],
            device_id=at_tgt(peer),
            device_id_type=MESH,
        )

    for d in range(1, tgt_n):
        sum_copy(d).start()

    @pl.loop(0, chunks)
    def _(c):
        for level in range(levels):
            each_copy(level, c, lambda k: k.wait_send())

    result = total[pl.ds(pl.multiple_of(tgt * piece, piece), piece), :]
    for d in range(1, tgt_n):
        sum_copy(d).wait()
        result = result + sums[d - 1]
    out[...] = result


def run(top_first, number, sizes, box, bits, patterns, targets, weights, state, evaluation):
    rows, width = state.shape
    levels = weights.shape[0]
    points = evaluation.shape[0]
    lower = (sizes[1] * sizes[3]).bit_length() - 2
    slots = max(lower, 1)
    chunks = rows // CHUNK
    others = max(sizes[2] - 1, 1)
    smem = pl.BlockSpec(memory_space=pltpu.SMEM)
    vmem = pl.BlockSpec(memory_space=pltpu.VMEM)
    return pl.pallas_call(
        partial(kernel, top_first, sizes),
        out_shape=jax.ShapeDtypeStruct((points // sizes[2], width), jnp.float32),
        in_specs=[smem, smem, vmem, vmem, vmem, vmem, pl.BlockSpec(memory_space=pl.ANY)],
        out_specs=vmem,
        scratch_shapes=[
            pltpu.VMEM((rows, width), jnp.bfloat16),
            pltpu.VMEM((levels, slots, rows, width), jnp.bfloat16),
            pltpu.VMEM((levels, 2, rows // GROUP, GROUP), jnp.float32),
            pltpu.VMEM((points, rows), jnp.bfloat16),
            pltpu.VMEM((points, width), jnp.float32),
            pltpu.VMEM((others, points // sizes[2], width), jnp.float32),
            pltpu.SemaphoreType.DMA((levels, slots, chunks)),
            pltpu.SemaphoreType.DMA((levels, slots, chunks)),
            pltpu.SemaphoreType.DMA,
            pltpu.SemaphoreType.DMA((others,)),
            pltpu.SemaphoreType.DMA((others,)),
        ],
        cost_estimate=pl.CostEstimate(
            flops=2 * levels * rows * weights.shape[1] * width, bytes_accessed=8 << 20, transcendentals=0),
        compiler_params=pltpu.CompilerParams(
            collective_id=number, has_side_effects=True, vmem_limit_bytes=40 << 20),
    )(box, bits, patterns, targets, weights, state, evaluation)


def body(sizes, coefficients, patterns, blocks, box_index, target_index, partner_bits, evaluation):
    state = coefficients[0]
    rows = state.shape[0]
    levels = patterns.shape[0]
    pattern_rows = patterns.reshape(levels, rows // GROUP, GROUP)
    targets = target_index.reshape(rows // GROUP, GROUP)

    grp_n = sizes[0]
    mine = lax.axis_index("grp")
    top = (sizes[1] * sizes[3]).bit_length() - 2

    def flag(bits):
        return (bits[0] == top).astype(jnp.int32)

    which = flag(partner_bits) << mine
    for apart in range(1, grp_n):
        theirs = lax.ppermute(partner_bits, "grp", [(g, (g + apart) % grp_n) for g in range(grp_n)])
        which = which + (flag(theirs) << ((mine - apart) % grp_n))
    variants = [tuple(bool(v >> g & 1) for g in range(grp_n)) for v in range(1 << grp_n)]
    result = lax.switch(
        which, [partial(run, variant, v, sizes) for v, variant in enumerate(variants)],
        box_index, partner_bits, pattern_rows, targets, blocks[:, 0], state, evaluation)
    return result[None]


def solution(mesh):
    sizes = tuple(mesh.shape[name] for name in ("grp", "bits", "tgt", "sub"))
    in_specs = (
        P(("grp", "bits", "sub"), "tgt", None),
        P(None, ("grp", "bits", "sub"), "tgt"),
        P(None, ("grp", "bits", "sub"), None, None),
        P(("grp", "bits", "sub")),
        P(("grp", "tgt")),
        P("grp"),
        P(),
    )
    out_specs = P(("grp", "bits", "sub"), "tgt", None)
    return jax.shard_map(
        partial(body, sizes), mesh=mesh, in_specs=in_specs, out_specs=out_specs, check_vma=False)
```

```python
from functools import partial
import math

import jax
import jax.numpy as jnp
from jax import lax
from jax.experimental import pallas as pl
from jax.experimental.pallas import tpu as pltpu
from jax.sharding import PartitionSpec as P

GROUP = 128
CHUNK = 256
LAG = 2
WINDOW = 3
MESH = pl.DeviceIdType.MESH


def column_of(row, rows, width):
    return jnp.transpose(jnp.broadcast_to(row, (width, rows)))


def cos_sin(turns):
    quarter = (turns + 512) >> 10
    x = (turns - (quarter << 10)).astype(jnp.float32) * (2.0 * math.pi / 4096.0)
    y = x * x
    s = x * (1.0 + y * (-1.0 / 6 + y * (1.0 / 120 + y * (-1.0 / 5040 + y * (1.0 / 362880)))))
    c = 1.0 + y * (-0.5 + y * (1.0 / 24 + y * (-1.0 / 720 + y * (1.0 / 40320 - y * (1.0 / 3628800)))))
    odd = (quarter & 1) == 1
    cos = jnp.where(odd, s, c)
    sin = jnp.where(odd, c, s)
    turn = quarter & 3
    cos = jnp.where((turn == 1) | (turn == 2), -cos, cos)
    sin = jnp.where((turn == 2) | (turn == 3), -sin, sin)
    return cos, sin


def mix(own, partner, pattern, weight, cos, sin):
    rows, width = own.shape
    terms = weight.shape[0] // width
    half = width // 2
    own32 = own.astype(jnp.float32)
    partner32 = partner.astype(jnp.float32)
    parts = []
    for k in range(terms):
        source = own32 if k < terms // 2 else partner32
        parts.append(jnp.where((pattern & (1 << k)) != 0, source, 0.0).astype(jnp.bfloat16))
    mixed = jnp.dot(jnp.concatenate(parts, axis=1), weight, preferred_element_type=jnp.float32)
    lane = lax.broadcasted_iota(jnp.int32, (rows, width), 1)
    signed = jnp.where(lane < half, -sin, sin)
    return (mixed * cos + pltpu.roll(mixed, half, 1) * signed).astype(jnp.bfloat16)


def kernel(top_first, sizes, box, bits, patterns, targets, weights_hbm, state_hbm, evaluation, out,
           state0, weights, state1, arrived, trig, points_eval, total, sums,
           send_sem, recv_sem, eval_sem, load_sem, sum_send, sum_recv):
    grp_n, bits_n, tgt_n, sub_n = sizes
    rows, width = state0.shape
    chunks = rows // CHUNK
    groups = CHUNK // GROUP
    levels = weights.shape[0]
    boxes = bits_n * sub_n
    lower = boxes.bit_length() - 2
    grp, tgt = lax.axis_index("grp"), lax.axis_index("tgt")
    me = lax.axis_index("bits") * sub_n + lax.axis_index("sub")
    if all(top_first):
        first = 1
    elif not any(top_first):
        first = 0
    else:
        first = sum(jnp.where(grp == g, 1, 0) for g in range(grp_n) if top_first[g])

    def across(stride):
        other = me + stride - 2 * stride * ((me // stride) % 2)
        return (grp, other // sub_n, tgt, other % sub_n)

    def at_tgt(t):
        return (grp, lax.axis_index("bits"), t, lax.axis_index("sub"))

    peers = [across(1 << j) for j in range(lower + 1)]
    peers += [at_tgt((tgt + d) % tgt_n) for d in range(1, tgt_n)]
    barrier = pltpu.get_barrier_semaphore()
    for peer in peers:
        pl.semaphore_signal(barrier, inc=1, device_id=peer, device_id_type=MESH)

    load_eval = pltpu.make_async_copy(
        evaluation.at[:, pl.ds(pl.multiple_of(tgt * rows, rows), rows)], points_eval, eval_sem)
    load_state = pltpu.make_async_copy(state_hbm, state0, load_sem.at[0])
    load_weights = pltpu.make_async_copy(weights_hbm, weights, load_sem.at[1])
    load_state.start()
    load_weights.start()
    load_eval.start()

    pl.semaphore_wait(barrier, len(peers))

    def is_top(level):
        return first if level == 0 else 1 - first

    def copy(level, slot, c):
        source = state_hbm if level == 0 else state1
        span = pl.ds(pl.multiple_of(c * CHUNK, CHUNK), CHUNK)
        stride = 1 << slot
        if slot == 0:
            stride = 1 + is_top(level) * ((1 << lower) - 1)
        return pltpu.make_async_remote_copy(
            src_ref=source.at[span],
            dst_ref=arrived.at[level, slot, span],
            send_sem=send_sem.at[level, slot, c],
            recv_sem=recv_sem.at[level, slot, c],
            device_id=across(stride),
            device_id_type=MESH,
        )

    def each_copy(level, c, act):
        act(copy(level, 0, c))
        top = is_top(level)
        if isinstance(top, int):
            if not top:
                for slot in range(1, lower):
                    act(copy(level, slot, c))
        elif lower > 1:
            @pl.when(top == 0)
            def _():
                for slot in range(1, lower):
                    act(copy(level, slot, c))

    @pl.loop(0, min(WINDOW, chunks))
    def _(c):
        each_copy(0, c, lambda k: k.start())

    for level in range(levels):
        turns = (targets[...] * (box[0] * (level + 1))) & 4095
        cos, sin = cos_sin(turns)
        trig[level, 0] = cos
        trig[level, 1] = sin
    total[...] = jnp.zeros_like(total)
    load_state.wait()
    load_weights.wait()
    load_eval.wait()

    def advance(level, c):
        each_copy(level, c, lambda k: k.wait_recv())
        if level == 0:
            @pl.when(c + WINDOW < chunks)
            def _():
                each_copy(0, c + WINDOW, lambda k: k.start())
        span = pl.ds(pl.multiple_of(c * CHUNK, CHUNK), CHUNK)
        own = (state0 if level == 0 else state1)[span, :]
        partner = arrived[level, 0, span, :]
        for slot in range(1, lower):
            partner = jnp.where(bits[level] == slot, arrived[level, slot, span, :], partner)

        def column(ref, *lead):
            return jnp.concatenate(
                [column_of(ref[(*lead, pl.ds(c * groups + g, 1), slice(None))], GROUP, width)
                 for g in range(groups)], axis=0)

        return mix(own, partner, column(patterns, level), weights[level],
                   column(trig, level, 0), column(trig, level, 1))

    @pl.loop(0, chunks + LAG)
    def _(i):
        @pl.when(i < chunks)
        def _():
            state1[pl.ds(pl.multiple_of(i * CHUNK, CHUNK), CHUNK), :] = advance(0, i)
            each_copy(1, i, lambda k: k.start())

        @pl.when(i >= LAG)
        def _():
            c = i - LAG
            span = pl.ds(pl.multiple_of(c * CHUNK, CHUNK), CHUNK)
            total[...] += jnp.dot(points_eval[:, span], advance(1, c), preferred_element_type=jnp.float32)

    piece = out.shape[0]

    def sum_copy(d):
        peer = (tgt + d) % tgt_n
        return pltpu.make_async_remote_copy(
            src_ref=total.at[pl.ds(pl.multiple_of(peer * piece, piece), piece)],
            dst_ref=sums.at[d - 1],
            send_sem=sum_send.at[d - 1],
            recv_sem=sum_recv.at[d - 1],
            device_id=at_tgt(peer),
            device_id_type=MESH,
        )

    for d in range(1, tgt_n):
        sum_copy(d).start()

    @pl.loop(0, chunks)
    def _(c):
        for level in range(levels):
            each_copy(level, c, lambda k: k.wait_send())

    result = total[pl.ds(pl.multiple_of(tgt * piece, piece), piece), :]
    for d in range(1, tgt_n):
        sum_copy(d).wait()
        result = result + sums[d - 1]
    out[...] = result


def run(top_first, number, sizes, box, bits, patterns, targets, weights, state, evaluation):
    rows, width = state.shape
    levels = weights.shape[0]
    points = evaluation.shape[0]
    lower = (sizes[1] * sizes[3]).bit_length() - 2
    slots = max(lower, 1)
    chunks = rows // CHUNK
    others = max(sizes[2] - 1, 1)
    smem = pl.BlockSpec(memory_space=pltpu.SMEM)
    vmem = pl.BlockSpec(memory_space=pltpu.VMEM)
    return pl.pallas_call(
        partial(kernel, top_first, sizes),
        out_shape=jax.ShapeDtypeStruct((points // sizes[2], width), jnp.float32),
        in_specs=[smem, smem, vmem, vmem] + [pl.BlockSpec(memory_space=pl.ANY)] * 3,
        out_specs=vmem,
        scratch_shapes=[
            pltpu.VMEM((rows, width), jnp.bfloat16),
            pltpu.VMEM(weights.shape, jnp.bfloat16),
            pltpu.VMEM((rows, width), jnp.bfloat16),
            pltpu.VMEM((levels, slots, rows, width), jnp.bfloat16),
            pltpu.VMEM((levels, 2, rows // GROUP, GROUP), jnp.float32),
            pltpu.VMEM((points, rows), jnp.bfloat16),
            pltpu.VMEM((points, width), jnp.float32),
            pltpu.VMEM((others, points // sizes[2], width), jnp.float32),
            pltpu.SemaphoreType.DMA((levels, slots, chunks)),
            pltpu.SemaphoreType.DMA((levels, slots, chunks)),
            pltpu.SemaphoreType.DMA,
            pltpu.SemaphoreType.DMA((2,)),
            pltpu.SemaphoreType.DMA((others,)),
            pltpu.SemaphoreType.DMA((others,)),
        ],
        cost_estimate=pl.CostEstimate(
            flops=2 * levels * rows * weights.shape[1] * width, bytes_accessed=8 << 20, transcendentals=0),
        compiler_params=pltpu.CompilerParams(
            collective_id=number, has_side_effects=True, vmem_limit_bytes=40 << 20),
    )(box, bits, patterns, targets, weights, state, evaluation)


def body(sizes, coefficients, patterns, blocks, box_index, target_index, partner_bits, evaluation):
    state = coefficients[0]
    rows = state.shape[0]
    levels = patterns.shape[0]
    pattern_rows = patterns.reshape(levels, rows // GROUP, GROUP)
    targets = target_index.reshape(rows // GROUP, GROUP)

    grp_n = sizes[0]
    mine = lax.axis_index("grp")
    top = (sizes[1] * sizes[3]).bit_length() - 2

    def flag(bits):
        return (bits[0] == top).astype(jnp.int32)

    which = flag(partner_bits) << mine
    for apart in range(1, grp_n):
        theirs = lax.ppermute(partner_bits, "grp", [(g, (g + apart) % grp_n) for g in range(grp_n)])
        which = which + (flag(theirs) << ((mine - apart) % grp_n))
    variants = [tuple(bool(v >> g & 1) for g in range(grp_n)) for v in range(1 << grp_n)]
    result = lax.switch(
        which, [partial(run, variant, v, sizes) for v, variant in enumerate(variants)],
        box_index, partner_bits, pattern_rows, targets, blocks[:, 0], state, evaluation)
    return result[None]


def solution(mesh):
    sizes = tuple(mesh.shape[name] for name in ("grp", "bits", "tgt", "sub"))
    in_specs = (
        P(("grp", "bits", "sub"), "tgt", None),
        P(None, ("grp", "bits", "sub"), "tgt"),
        P(None, ("grp", "bits", "sub"), None, None),
        P(("grp", "bits", "sub")),
        P(("grp", "tgt")),
        P("grp"),
        P(),
    )
    out_specs = P(("grp", "bits", "sub"), "tgt", None)
    return jax.shard_map(
        partial(body, sizes), mesh=mesh, in_specs=in_specs, out_specs=out_specs, check_vma=False)
```

```python
from functools import partial
import math

import jax
import jax.numpy as jnp
from jax import lax
from jax.experimental import pallas as pl
from jax.experimental.pallas import tpu as pltpu
from jax.sharding import PartitionSpec as P

GROUP = 128
CHUNK = 256
LAG = 2
WINDOW = 3
MESH = pl.DeviceIdType.MESH


def column_of(row, rows, width):
    return jnp.transpose(jnp.broadcast_to(row, (width, rows)))


def cos_sin(turns):
    quarter = (turns + 512) >> 10
    x = (turns - (quarter << 10)).astype(jnp.float32) * (2.0 * math.pi / 4096.0)
    y = x * x
    s = x * (1.0 + y * (-1.0 / 6 + y * (1.0 / 120 + y * (-1.0 / 5040 + y * (1.0 / 362880)))))
    c = 1.0 + y * (-0.5 + y * (1.0 / 24 + y * (-1.0 / 720 + y * (1.0 / 40320 - y * (1.0 / 3628800)))))
    odd = (quarter & 1) == 1
    cos = jnp.where(odd, s, c)
    sin = jnp.where(odd, c, s)
    turn = quarter & 3
    cos = jnp.where((turn == 1) | (turn == 2), -cos, cos)
    sin = jnp.where((turn == 2) | (turn == 3), -sin, sin)
    return cos, sin


def mix(own, partner, pattern, weight, cos, sin):
    rows, width = own.shape
    terms = weight.shape[0] // width
    half = width // 2
    own32 = own.astype(jnp.float32)
    partner32 = partner.astype(jnp.float32)
    parts = []
    for k in range(terms):
        source = own32 if k < terms // 2 else partner32
        parts.append(jnp.where((pattern & (1 << k)) != 0, source, 0.0).astype(jnp.bfloat16))
    mixed = jnp.dot(jnp.concatenate(parts, axis=1), weight, preferred_element_type=jnp.float32)
    lane = lax.broadcasted_iota(jnp.int32, (rows, width), 1)
    signed = jnp.where(lane < half, -sin, sin)
    return (mixed * cos + pltpu.roll(mixed, half, 1) * signed).astype(jnp.bfloat16)


def kernel(top_first, sizes, box, bits, patterns, targets, weights_hbm, state_hbm, evaluation, out,
           state0, weights, state1, arrived, trig, points_eval, total, sums,
           send_sem, recv_sem, eval_sem, load_sem, sum_send, sum_recv):
    grp_n, bits_n, tgt_n, sub_n = sizes
    rows, width = state0.shape
    chunks = rows // CHUNK
    groups = CHUNK // GROUP
    levels = weights.shape[0]
    boxes = bits_n * sub_n
    lower = boxes.bit_length() - 2
    grp, tgt = lax.axis_index("grp"), lax.axis_index("tgt")
    me = lax.axis_index("bits") * sub_n + lax.axis_index("sub")
    if all(top_first):
        first = 1
    elif not any(top_first):
        first = 0
    else:
        first = sum(jnp.where(grp == g, 1, 0) for g in range(grp_n) if top_first[g])

    def across(stride):
        other = me + stride - 2 * stride * ((me // stride) % 2)
        return (grp, other // sub_n, tgt, other % sub_n)

    def at_tgt(t):
        return (grp, lax.axis_index("bits"), t, lax.axis_index("sub"))

    peers = [across(1 << j) for j in range(lower + 1)]
    peers += [at_tgt((tgt + d) % tgt_n) for d in range(1, tgt_n)]
    barrier = pltpu.get_barrier_semaphore()
    for peer in peers:
        pl.semaphore_signal(barrier, inc=1, device_id=peer, device_id_type=MESH)

    load_eval = pltpu.make_async_copy(
        evaluation.at[:, pl.ds(pl.multiple_of(tgt * rows, rows), rows)], points_eval, eval_sem)
    load_state = pltpu.make_async_copy(state_hbm, state0, load_sem.at[0])
    load_weights = pltpu.make_async_copy(weights_hbm, weights, load_sem.at[1])
    load_state.start()
    load_weights.start()
    load_eval.start()

    pl.semaphore_wait(barrier, len(peers))

    def is_top(level):
        return first if level == 0 else 1 - first

    def copy(level, slot, c):
        source = state_hbm if level == 0 else state1
        span = pl.ds(pl.multiple_of(c * CHUNK, CHUNK), CHUNK)
        stride = 1 << slot
        if slot == 0:
            stride = 1 + is_top(level) * ((1 << lower) - 1)
        return pltpu.make_async_remote_copy(
            src_ref=source.at[span],
            dst_ref=arrived.at[level, slot, span],
            send_sem=send_sem.at[level, slot, c],
            recv_sem=recv_sem.at[level, slot, c],
            device_id=across(stride),
            device_id_type=MESH,
        )

    def each_copy(level, c, act):
        act(copy(level, 0, c))
        top = is_top(level)
        if isinstance(top, int):
            if not top:
                for slot in range(1, lower):
                    act(copy(level, slot, c))
        elif lower > 1:
            @pl.when(top == 0)
            def _():
                for slot in range(1, lower):
                    act(copy(level, slot, c))

    @pl.loop(0, min(WINDOW, chunks))
    def _(c):
        each_copy(0, c, lambda k: k.start())

    for level in range(levels):
        turns = (targets[...] * (box[0] * (level + 1))) & 4095
        cos, sin = cos_sin(turns)
        trig[level, 0] = cos
        trig[level, 1] = sin
    total[...] = jnp.zeros_like(total)
    load_state.wait()
    load_weights.wait()
    load_eval.wait()

    def advance(level, c):
        each_copy(level, c, lambda k: k.wait_recv())
        if level == 0:
            @pl.when(c + WINDOW < chunks)
            def _():
                each_copy(0, c + WINDOW, lambda k: k.start())
        span = pl.ds(pl.multiple_of(c * CHUNK, CHUNK), CHUNK)
        own = (state0 if level == 0 else state1)[span, :]
        partner = arrived[level, 0, span, :]
        for slot in range(1, lower):
            partner = jnp.where(bits[level] == slot, arrived[level, slot, span, :], partner)

        def column(ref, *lead):
            return jnp.concatenate(
                [column_of(ref[(*lead, pl.ds(c * groups + g, 1), slice(None))], GROUP, width)
                 for g in range(groups)], axis=0)

        return mix(own, partner, column(patterns, level), weights[level],
                   column(trig, level, 0), column(trig, level, 1))

    @pl.loop(0, chunks + LAG)
    def _(i):
        @pl.when(i < chunks)
        def _():
            state1[pl.ds(pl.multiple_of(i * CHUNK, CHUNK), CHUNK), :] = advance(0, i)
            each_copy(1, i, lambda k: k.start())
            each_copy(0, i, lambda k: k.wait_send())

        @pl.when(i >= LAG)
        def _():
            c = i - LAG
            span = pl.ds(pl.multiple_of(c * CHUNK, CHUNK), CHUNK)
            total[...] += jnp.dot(points_eval[:, span], advance(1, c), preferred_element_type=jnp.float32)
            each_copy(1, c, lambda k: k.wait_send())

    piece = out.shape[0]

    def sum_copy(d):
        peer = (tgt + d) % tgt_n
        return pltpu.make_async_remote_copy(
            src_ref=total.at[pl.ds(pl.multiple_of(peer * piece, piece), piece)],
            dst_ref=sums.at[d - 1],
            send_sem=sum_send.at[d - 1],
            recv_sem=sum_recv.at[d - 1],
            device_id=at_tgt(peer),
            device_id_type=MESH,
        )

    for d in range(1, tgt_n):
        sum_copy(d).start()

    result = total[pl.ds(pl.multiple_of(tgt * piece, piece), piece), :]
    for d in range(1, tgt_n):
        sum_copy(d).wait()
        result = result + sums[d - 1]
    out[...] = result


def run(top_first, number, sizes, box, bits, patterns, targets, weights, state, evaluation):
    rows, width = state.shape
    levels = weights.shape[0]
    points = evaluation.shape[0]
    lower = (sizes[1] * sizes[3]).bit_length() - 2
    slots = max(lower, 1)
    chunks = rows // CHUNK
    others = max(sizes[2] - 1, 1)
    smem = pl.BlockSpec(memory_space=pltpu.SMEM)
    vmem = pl.BlockSpec(memory_space=pltpu.VMEM)
    return pl.pallas_call(
        partial(kernel, top_first, sizes),
        out_shape=jax.ShapeDtypeStruct((points // sizes[2], width), jnp.float32),
        in_specs=[smem, smem, vmem, vmem] + [pl.BlockSpec(memory_space=pl.ANY)] * 3,
        out_specs=vmem,
        scratch_shapes=[
            pltpu.VMEM((rows, width), jnp.bfloat16),
            pltpu.VMEM(weights.shape, jnp.bfloat16),
            pltpu.VMEM((rows, width), jnp.bfloat16),
            pltpu.VMEM((levels, slots, rows, width), jnp.bfloat16),
            pltpu.VMEM((levels, 2, rows // GROUP, GROUP), jnp.float32),
            pltpu.VMEM((points, rows), jnp.bfloat16),
            pltpu.VMEM((points, width), jnp.float32),
            pltpu.VMEM((others, points // sizes[2], width), jnp.float32),
            pltpu.SemaphoreType.DMA((levels, slots, chunks)),
            pltpu.SemaphoreType.DMA((levels, slots, chunks)),
            pltpu.SemaphoreType.DMA,
            pltpu.SemaphoreType.DMA((2,)),
            pltpu.SemaphoreType.DMA((others,)),
            pltpu.SemaphoreType.DMA((others,)),
        ],
        cost_estimate=pl.CostEstimate(
            flops=2 * levels * rows * weights.shape[1] * width, bytes_accessed=8 << 20, transcendentals=0),
        compiler_params=pltpu.CompilerParams(
            collective_id=number, has_side_effects=True, vmem_limit_bytes=40 << 20),
    )(box, bits, patterns, targets, weights, state, evaluation)


def body(sizes, coefficients, patterns, blocks, box_index, target_index, partner_bits, evaluation):
    state = coefficients[0]
    rows = state.shape[0]
    levels = patterns.shape[0]
    pattern_rows = patterns.reshape(levels, rows // GROUP, GROUP)
    targets = target_index.reshape(rows // GROUP, GROUP)

    grp_n = sizes[0]
    mine = lax.axis_index("grp")
    top = (sizes[1] * sizes[3]).bit_length() - 2

    def flag(bits):
        return (bits[0] == top).astype(jnp.int32)

    which = flag(partner_bits) << mine
    for apart in range(1, grp_n):
        theirs = lax.ppermute(partner_bits, "grp", [(g, (g + apart) % grp_n) for g in range(grp_n)])
        which = which + (flag(theirs) << ((mine - apart) % grp_n))
    variants = [tuple(bool(v >> g & 1) for g in range(grp_n)) for v in range(1 << grp_n)]
    result = lax.switch(
        which, [partial(run, variant, v, sizes) for v, variant in enumerate(variants)],
        box_index, partner_bits, pattern_rows, targets, blocks[:, 0], state, evaluation)
    return result[None]


def solution(mesh):
    sizes = tuple(mesh.shape[name] for name in ("grp", "bits", "tgt", "sub"))
    in_specs = (
        P(("grp", "bits", "sub"), "tgt", None),
        P(None, ("grp", "bits", "sub"), "tgt"),
        P(None, ("grp", "bits", "sub"), None, None),
        P(("grp", "bits", "sub")),
        P(("grp", "tgt")),
        P("grp"),
        P(),
    )
    out_specs = P(("grp", "bits", "sub"), "tgt", None)
    return jax.shard_map(
        partial(body, sizes), mesh=mesh, in_specs=in_specs, out_specs=out_specs, check_vma=False)
```
